256 devices in a mesh: ctx: 64 (over x, z, core), head: 4 (over y).
Axes of the slice: x: 4, y: 4, z: 8, core: 2. Of those that a mesh axis runs over, the one named last changes fastest.
Arguments:
- lin_q: bfloat16 [8192, 64, 128], P('ctx', 'head'), may hold values from -6 to 6
- lin_k: bfloat16 [8192, 64, 128], P('ctx', 'head'), may hold values from -0.5 to 0.5
- lin_v: bfloat16 [8192, 64, 128], P('ctx', 'head'), may hold values from -6 to 6
- decay_rate: float32 [64], P('head'), may hold values from 2.4414062e-06 to 0.03
- norm_gain: float32 [64, 128], P('head'), may hold values from 0.1 to 1.9
- soft_q: bfloat16 [8192, 64, 128], P('ctx', 'head'), may hold values from -6 to 6
- soft_k: bfloat16 [8192, 8, 128], P('ctx', 'head'), may hold values from -6 to 6
- soft_v: bfloat16 [8192, 8, 128], P('ctx', 'head'), may hold values from -6 to 6
- doc_ids: int32 [64], P('ctx'), may hold values from 0 to 7, never falling along the last dimension, each value on 1 to 32 neighbouring positions
- block_mask: int32 [64, 64], P('ctx'), may hold values 0 or 1
Outputs:
- lin_out: bfloat16 [8192, 64, 128], P('ctx', 'head')
- soft_out: bfloat16 [8192, 64, 128], P('ctx', 'head')
The draws below stay inside these ranges and needn't reach their ends.
Inputs may be any that keep to these rules, and one draw needn't show every extreme that they name: `doc_ids`: document ids never fall along the sequence; each document covers 1 to 32 whole tiles, and one covers exactly 32.
All inputs are finite; a program needn't handle non-finite values. No bound on the sum of `block_mask` on one device may be relied on, other than what follows from the above.
Results may differ from the reference program's by a relative error of at most 0.0045.
Values may be sent and summed in bfloat16 or wider, within the bound.
No kernel may reach another device: no remote copies, remote signals or barrier semaphores. Data moves between devices by JAX's collectives and lax.ppermute only.
A program may use at most 320 MiB of HBM per device.

```python
import math
import jax
import jax.numpy as jnp
import numpy as np
from jax import lax

HEAD_DIM = 128
HEADS = 64
KV_HEADS = 8
TILE = 128
SEQ = 8192
TILES = 64
DOC_TILES = 32
DOCS = 8


def soft_pair(key):
    key_q, key_k = jax.random.split(jax.random.fold_in(key, 7), 2)
    queries = jnp.clip(jax.random.normal(key_q, (SEQ, HEADS, HEAD_DIM), jnp.float32), -6.0, 6.0)
    keys = jnp.clip(jax.random.normal(key_k, (SEQ, KV_HEADS, HEAD_DIM), jnp.float32), -6.0, 6.0)
    return (queries, keys)


def draw_soft_q(key, part):
    return soft_pair(key)[0].astype(jnp.bfloat16)


def draw_soft_k(key, part):
    return soft_pair(key)[1].astype(jnp.bfloat16)


def with_ends(array, stream_key, smallest, high):
    longest = array.shape.index(max(array.shape))
    spots = []
    for shift in (0, 1):
        where = [jax.random.randint(jax.random.fold_in(stream_key, axis), (), 0, length) for axis, length in enumerate(array.shape)]
        where[longest] = (where[longest] + shift) % array.shape[longest]
        spots.append(tuple(where))
    return array.at[spots[0]].set(smallest).at[spots[1]].set(high)


def shard_levels(rng, extent, cuts, smallest, largest):
    loudness, own = 1.0, jax.random.fold_in(rng, 6)
    for axis_at, parts in cuts:
        heights = jnp.exp(jax.random.uniform(jax.random.fold_in(own, axis_at), (parts,), jnp.float32, smallest / len(cuts), largest / len(cuts)))
        loudness = loudness * jnp.repeat(heights, extent[axis_at] // parts).reshape([-1 if axis == axis_at else 1 for axis in range(len(extent))])
    return loudness


def profile(number_of, total, most, slope):
    portions = [(1 << 20) // math.isqrt(rank ** slope) + 1 for rank in range(2, number_of + 1)]
    surplus, given = total - most - (number_of - 1), [1] * (number_of - 1)
    while surplus > 0:
        candidates = [i for i in range(number_of - 1) if given[i] < most]
        pool, left = sum([portions[i] for i in candidates]), surplus
        for i in candidates:
            extra = min(most - given[i], max(1, left * portions[i] // pool), surplus)
            given[i] = given[i] + extra
            surplus = surplus - extra
    return np.array([most] + given)


def uneven(key, number_of, total, bound, skew):
    if number_of == 2:
        one = jax.random.randint(key, (), max(1, total - bound), min(bound, total - 1) + 1)
        return jnp.stack([one, total - one])
    lengths = jnp.asarray(profile(number_of, total, bound, skew), jnp.int32)
    couples = (number_of - 1) // 2
    donor, taker = lengths[1:1 + 2 * couples:2], lengths[2:2 + 2 * couples:2]
    slack = jnp.minimum(donor - 1, bound - taker)
    moved = jax.random.randint(jax.random.fold_in(key, 1), (couples,), 0, 1 << 20) % (slack + 1)
    lengths = lengths.at[1:1 + 2 * couples:2].set(donor - moved).at[2:2 + 2 * couples:2].set(taker + moved)
    return lengths[jax.random.permutation(jax.random.fold_in(key, 2), number_of)]


def noise(rng, shape, deviation, bound, shards=(), dtype=jnp.bfloat16):
    array = deviation * jax.random.normal(rng, shape, jnp.float32)
    if shards:
        array = array * shard_levels(rng, shape, shards, -0.22, 0.18)
    return jnp.clip(array, -bound, bound).astype(dtype)


def setup_inputs(seed: int = 0) -> dict:
    arg_keys = jax.random.split(jax.random.key(seed), 11)
    return {
        "lin_q": noise(arg_keys[0], (SEQ, HEADS, HEAD_DIM), 1.0, 6.0, ((0, 64), (1, 4))),
        "lin_k": noise(arg_keys[1], (SEQ, HEADS, HEAD_DIM), HEAD_DIM ** -0.5, 0.5, ((0, 64), (1, 4))),
        "lin_v": noise(arg_keys[2], (SEQ, HEADS, HEAD_DIM), 1.0, 6.0, ((0, 64), (1, 4))),
        "decay_rate": jnp.clip(jnp.exp(math.log(0.03) - 9.416378 * jax.random.uniform(arg_keys[3], (HEADS,), jnp.float32) ** shard_levels(arg_keys[3], (HEADS,), ((0, 4),), -0.2, 0.2)), 2.441406195430318e-06, 0.03),
        "norm_gain": jnp.clip(1.0 + 0.18 * jax.random.normal(arg_keys[4], (HEADS, HEAD_DIM), jnp.float32), 0.1, 1.9),
        "soft_q": draw_soft_q(jax.random.fold_in(arg_keys[10], 71), 0),
        "soft_k": draw_soft_k(jax.random.fold_in(arg_keys[10], 71), 0),
        "soft_v": noise(arg_keys[7], (SEQ, KV_HEADS, HEAD_DIM), 1.0, 6.0, ((0, 64), (1, 4))),
        "doc_ids": jnp.searchsorted(jnp.cumsum(uneven(arg_keys[8], DOCS, TILES, DOC_TILES, 2)), jnp.arange(TILES), side="right").astype(jnp.int32),
        "block_mask": with_ends((jax.random.randint(arg_keys[9], (TILES, TILES), 0, 2) < 1).astype(jnp.int32), jax.random.fold_in(arg_keys[9], 1), 0, 1),
    }


def lightning(lin_q, lin_k, lin_v, decay_rate):
    highest = lax.Precision.HIGHEST
    blocks_q = lin_q.astype(jnp.float32).reshape(TILES, TILE, HEADS, HEAD_DIM)
    blocks_k = lin_k.astype(jnp.float32).reshape(TILES, TILE, HEADS, HEAD_DIM)
    blocks_v = lin_v.astype(jnp.float32).reshape(TILES, TILE, HEADS, HEAD_DIM)
    rate = decay_rate.astype(jnp.float32)
    position = jnp.arange(TILE).astype(jnp.float32)
    distance = position[:, None] - position[None, :]
    within = jnp.where((distance >= 0)[None], jnp.exp(-rate[:, None, None] * jnp.maximum(distance, 0.0)[None]), 0.0)
    tail = jnp.exp(-rate[None, :] * (TILE - position)[:, None])
    head_decay = jnp.exp(-rate[None, :] * position[:, None])
    block_decay = jnp.exp(-rate * TILE)

    def advance(state, block):
        query, keys, values = block
        scores = jnp.einsum('thd,shd->hts', query, keys, precision=highest) * within
        inner = jnp.einsum('hts,she->the', scores, values, precision=highest)
        outer = jnp.einsum('thd,hde->the', query * head_decay[:, :, None], state, precision=highest)
        local_state = jnp.einsum('shd,she->hde', keys * tail[:, :, None], values, precision=highest)
        return (block_decay[:, None, None] * state + local_state, inner + outer)
    start = jnp.zeros((HEADS, HEAD_DIM, HEAD_DIM), jnp.float32)
    _, mixed = lax.scan(advance, start, (blocks_q, blocks_k, blocks_v))
    return mixed.reshape(SEQ, HEADS, HEAD_DIM)

def softmax_layer(soft_q, soft_k, soft_v, doc_ids, block_mask):
    groups = HEADS // KV_HEADS
    window = DOC_TILES * TILE
    scale_factor = 1.0 / HEAD_DIM ** 0.5

    def one_tile(tile_index):
        first = jnp.maximum(tile_index - DOC_TILES + 1, 0).astype(jnp.int32) * TILE
        query = lax.dynamic_slice_in_dim(soft_q, (tile_index * TILE).astype(jnp.int32), TILE, 0)
        query = query.astype(jnp.float32).reshape(TILE, KV_HEADS, groups, HEAD_DIM)
        keys = lax.dynamic_slice_in_dim(soft_k, first, window, 0).astype(jnp.float32)
        values = lax.dynamic_slice_in_dim(soft_v, first, window, 0).astype(jnp.float32)
        key_pos = first + jnp.arange(window).astype(jnp.int32)
        query_pos = tile_index * TILE + jnp.arange(TILE).astype(jnp.int32)
        key_tile = key_pos // TILE
        mask_row = jnp.take(block_mask, tile_index, axis=0)
        tile_ok = ((jnp.take(mask_row, key_tile) == 1) | (key_tile == tile_index)) & (jnp.take(doc_ids, key_tile) == jnp.take(doc_ids, tile_index))
        allowed = tile_ok[None, :] & (key_pos[None, :] <= query_pos[:, None])
        scores = jnp.einsum('tkgd,skd->kgts', query, keys) * scale_factor
        masked = jnp.where(allowed, scores, -1e+30)
        peak = lax.optimization_barrier(jnp.max(masked, axis=-1, keepdims=True))
        weights = jnp.where(allowed, jnp.exp(masked - peak), 0.0)
        total = lax.optimization_barrier(jnp.sum(weights, axis=-1))
        rounded = weights.astype(jnp.bfloat16).astype(jnp.float32)
        summed = jnp.einsum('kgts,skd->tkgd', rounded, values)
        result = summed / jnp.transpose(total, (2, 0, 1))[..., None]
        return result.reshape(TILE, HEADS, HEAD_DIM).astype(jnp.bfloat16)
    tiles_out = lax.map(one_tile, jnp.arange(TILES).astype(jnp.int32))
    return tiles_out.reshape(SEQ, HEADS, HEAD_DIM)

def reference(lin_q, lin_k, lin_v, decay_rate, norm_gain, soft_q, soft_k, soft_v, doc_ids, block_mask):
    mixed = lightning(lin_q, lin_k, lin_v, decay_rate)
    mean_square = lax.optimization_barrier(jnp.mean(mixed * mixed, axis=(1, 2)))
    lin_out = (mixed * lax.rsqrt(mean_square + 1e-05)[:, None, None] * norm_gain[None]).astype(jnp.bfloat16)
    soft_out = softmax_layer(soft_q, soft_k, soft_v, doc_ids, block_mask)
    return (lin_out, soft_out)
```

```python
import functools

import jax
import jax.numpy as jnp
from jax import lax
from jax.experimental import pallas as pl
from jax.experimental.pallas import tpu as pltpu
from jax.sharding import Mesh, PartitionSpec as P

D = 128
TILE = 128
HEADS = 64
LOCAL = 16
KV = 2
GROUPS = 8
ROWS = TILE * GROUPS
BLOCK = 4 * TILE + 16
CHUNK = 256
SCALE = 1.4426950408889634 / D**0.5
LOWEST = -1e30
bf16, f32 = jnp.bfloat16, jnp.float32
CHIPS = ("x", "zh", "zl")
VMEM = pl.BlockSpec(memory_space=pltpu.VMEM)
SMEM = pl.BlockSpec(memory_space=pltpu.SMEM)


def dot(a, b, ca=1, cb=0):
    return lax.dot_general(a, b, (((ca,), (cb,)), ((), ())), preferred_element_type=f32)


def split(value):
    high = value.astype(bf16)
    return high, (value - high.astype(f32)).astype(bf16)


def iota(shape, axis):
    return lax.broadcasted_iota(jnp.int32, shape, axis)


def call(body, outs, ins, scratch=(), flops=0, nbytes=4 << 20):
    return pl.pallas_call(
        body,
        out_shape=outs,
        in_specs=ins,
        out_specs=jax.tree.map(lambda _: VMEM, outs),
        scratch_shapes=list(scratch),
        compiler_params=pltpu.CompilerParams(vmem_limit_bytes=40 << 20),
        cost_estimate=pl.CostEstimate(flops=flops, bytes_accessed=nbytes, transcendentals=0),
    )


def shape(dims, dtype):
    return jax.ShapeDtypeStruct(dims, dtype)


def flash_body(first, last, groups, *refs):
    refs = list(refs)
    place, doc, mask = refs[:3]
    blocks = refs[3 : 3 + len(groups)]
    refs = refs[3 + len(groups) :]
    if first:
        q_in, own = refs[:2]
        refs = refs[2:]
    else:
        qt, peak_in, total_in, acc_in = refs[:4]
        refs = refs[4:]
    if last:
        out = refs[0]
        refs = refs[1:]
        kbuf, vbuf, peak, total, acc = refs
    elif first:
        qt, peak, total, acc, kbuf, vbuf = refs
    else:
        peak, total, acc, kbuf, vbuf = refs

    chip, core = place[0], place[1]
    mine = 2 * chip + core

    def attend(h, keys, values_t, causal):
        for c in range(ROWS // CHUNK):
            cols = slice(c * CHUNK, (c + 1) * CHUNK)
            s = dot(keys, qt[h, :, cols])
            if causal:
                keep = iota(s.shape, 0) <= (c * CHUNK + iota(s.shape, 1)) // GROUPS
                s = jnp.where(keep, s, LOWEST)
                top = jnp.max(s, axis=0, keepdims=True)
                p = jnp.exp2((s - top) * SCALE)
                total[h, :, cols] = jnp.sum(p, axis=0, keepdims=True)
                acc[h, :, cols] = dot(values_t, p.astype(bf16))
            else:
                old = peak[h, :, cols]
                top = jnp.maximum(old, jnp.max(s, axis=0, keepdims=True))
                fade = jnp.exp2((old - top) * SCALE)
                p = jnp.exp2((s - top) * SCALE)
                total[h, :, cols] = total[h, :, cols] * fade + jnp.sum(p, axis=0, keepdims=True)
                acc[h, :, cols] = acc[h, :, cols] * fade + dot(values_t, p.astype(bf16))
            peak[h, :, cols] = top

    if first:
        q = q_in[...].astype(f32)
        for h in range(KV):
            qt[h] = q[:, h * GROUPS : (h + 1) * GROUPS, :].reshape(ROWS, D).T.astype(bf16)
        for h in range(KV):
            attend(h, own[h * D : (h + 1) * D], own[(KV + h) * D : (KV + h + 1) * D], True)
    else:
        peak[...] = peak_in[...]
        total[...] = total_in[...]
        acc[...] = acc_in[...]

    entries = [(r, i, dist, other) for r, (dists, other) in enumerate(groups) for i, dist in enumerate(dists)]
    docs = jnp.concatenate([blocks[r][i, 4 * D : 4 * D + 16, :].astype(f32)[0:1] for r, i, _, _ in entries], axis=0)
    weight = jnp.left_shift(1, iota(docs.shape, 0)).astype(f32)
    same = (docs == doc[0].astype(f32)) & (iota(docs.shape, 1) == 0)
    bits = jnp.sum(jnp.where(same, weight, 0.0)).astype(jnp.int32)
    count = jnp.int32(0)
    for n, (r, i, dist, other) in enumerate(entries):
        tile = 2 * (chip - dist) + (1 - core if other else core)
        ok = (jnp.bitwise_and(lax.shift_right_logical(bits, n), 1) == 1) & (tile >= 0) & (tile < mine)
        ok = ok & (mask[0, jnp.maximum(tile, 0)] == 1)

        @pl.when(ok)
        def _(r=r, i=i, count=count):
            for h in range(KV):
                kbuf[h, count] = blocks[r][i, h * D : (h + 1) * D, :]
                vbuf[h, count] = blocks[r][i, (KV + h) * D : (KV + h + 1) * D, :]

        count = count + ok.astype(jnp.int32)

    def pair(n, carry):
        for h in range(KV):
            keys = jnp.concatenate([kbuf[h, 2 * n], kbuf[h, 2 * n + 1]], axis=0)
            values_t = jnp.concatenate([vbuf[h, 2 * n], vbuf[h, 2 * n + 1]], axis=1)
            attend(h, keys, values_t, False)
        return carry

    lax.fori_loop(0, lax.shift_right_logical(count, 1), pair, 0)

    @pl.when(jnp.bitwise_and(count, 1) == 1)
    def _():
        for h in range(KV):
            attend(h, kbuf[h, count - 1], vbuf[h, count - 1], False)

    if last:
        heads = [(acc[h] / total[h]).T.reshape(TILE, GROUPS, D) for h in range(KV)]
        out[...] = jnp.concatenate(heads, axis=1).astype(bf16)


def flash(place, doc, mask, blocks, groups, first=None, state=None, last=False):
    state_shapes = [shape((KV, 1, ROWS), f32), shape((KV, 1, ROWS), f32), shape((KV, D, ROWS), f32)]
    slots = sum(len(dists) for dists, _ in groups)
    buffers = [pltpu.VMEM((KV, slots, D, D), bf16)] * 2
    if last:
        outs = shape((TILE, LOCAL, D), bf16)
        scratch = buffers + [pltpu.VMEM(s.shape, s.dtype) for s in state_shapes]
    else:
        outs = state_shapes
        scratch = buffers
    if first is not None:
        outs = [shape((KV, D, ROWS), bf16)] + outs
        extra = list(first)
    else:
        extra = list(state)
    body = functools.partial(flash_body, first is not None, last, groups)
    return call(body, outs, [SMEM] * 3 + [VMEM] * (len(blocks) + len(extra)), scratch, flops=slots * (1 << 28))(
        place, doc, mask, *blocks, *extra
    )


def state_body(rate, k_in, v_in, high_out, state_out, kf, vf):
    kf[...] = k_in[...].astype(f32).reshape(TILE * LOCAL, D)
    vf[...] = v_in[...].astype(f32).reshape(TILE * LOCAL, D)
    left = (TILE - iota((TILE, D), 0)).astype(f32)
    for h in range(LOCAL):
        keys = kf[pl.ds(h, TILE, stride=LOCAL), :] * jnp.exp(-rate[h] * left)
        values = vf[pl.ds(h, TILE, stride=LOCAL), :].astype(bf16)
        high, low = split(keys)
        state = dot(high, values, 0, 0) + dot(low, values, 0, 0)
        state_out[h] = state
        high_out[h] = state.astype(bf16)


def inner_body(rate, q_in, k_in, v_in, inner_out, q_out, qf, kf, vf):
    qf[...] = q_in[...].astype(f32).reshape(TILE * LOCAL, D)
    kf[...] = k_in[...].astype(f32).reshape(TILE * LOCAL, D)
    vf[...] = v_in[...].astype(f32).reshape(TILE * LOCAL, D)
    distance = iota((TILE, TILE), 0) - iota((TILE, TILE), 1)
    steps = jnp.maximum(distance, 0).astype(f32)
    for h in range(LOCAL):
        query = qf[pl.ds(h, TILE, stride=LOCAL), :].astype(bf16)
        keys = kf[pl.ds(h, TILE, stride=LOCAL), :].astype(bf16)
        values = vf[pl.ds(h, TILE, stride=LOCAL), :].astype(bf16)
        within = jnp.where(distance >= 0, jnp.exp(-rate[h] * steps), 0.0)
        high, low = split(dot(query, keys, 1, 1) * within)
        inner_out[h] = dot(high, values) + dot(low, values)
        q_out[h] = query


def outer_body(place, rate, inner, q, near, far, before, mixed_out, sums_out, squares):
    core = place[1]
    upper = core == 1
    position = iota((TILE, D), 0).astype(f32)
    squares[...] = jnp.zeros_like(squares)
    for half, source in ((core, near), (1 - core, far)):
        for i in range(LOCAL // 2):
            h = half * (LOCAL // 2) + i
            r = rate[h]
            fade = jnp.exp(jnp.full((1, D), -TILE, f32) * r)
            entering = source[i].astype(f32)
            entering = jnp.where(upper, fade * entering + before[h].astype(f32), entering)
            high, low = split(entering)
            query = q[h]
            outer = (dot(query, high) + dot(query, low)) * jnp.exp(-r * position)
            mixed = inner[h] + outer
            mixed_out[h] = mixed
            squares[...] += mixed * mixed
    sums_out[...] = jnp.broadcast_to(jnp.sum(squares[...].T, axis=0, keepdims=True), (8, TILE))


def norm_body(mixed, own, s1, s2, s3, gain, out, rows):
    sums = own[...] + s1[...] + s2[...] + s3[...]
    inverse = lax.rsqrt(sums / (HEADS * D) + 1e-5)
    inverse = jnp.broadcast_to(inverse[0:1], (D, TILE)).T
    for h in range(LOCAL):
        rows[pl.ds(h, TILE, stride=LOCAL), :] = mixed[h] * inverse * gain[h : h + 1, :]
    out[...] = rows[...].reshape(TILE, LOCAL, D).astype(bf16)


def chip_shift(value, steps):
    return lax.ppermute(value, CHIPS, [(i, (i + steps) % 32) for i in range(32)])


def x_shift(value, steps):
    return lax.ppermute(value, "x", [(i, (i + steps) % 4) for i in range(4)])


def head_shift(value, steps):
    return lax.ppermute(value, "head", [(i, (i + steps) % 4) for i in range(4)])


def swap(value, axis="core"):
    return lax.ppermute(value, axis, [(0, 1), (1, 0)])


def on_device(lin_q, lin_k, lin_v, decay_rate, norm_gain, soft_q, soft_k, soft_v, doc_ids, block_mask):
    x, zh, zl, core = (lax.axis_index(a) for a in ("x", "zh", "zl", "core"))
    chip = (x * 2 + zh) * 4 + zl
    place = jnp.stack([chip, core]).astype(jnp.int32)
    big = pltpu.VMEM((TILE * LOCAL, D), f32)
    heads = (LOCAL, D, D)

    state_high, state = call(
        state_body, [shape(heads, bf16), shape(heads, f32)], [SMEM, VMEM, VMEM], [big, big], flops=1 << 27
    )(decay_rate, lin_k, lin_v)

    block = jnp.concatenate(
        [
            jnp.transpose(soft_k, (1, 0, 2)).reshape(KV * D, D),
            jnp.transpose(soft_v, (1, 2, 0)).reshape(KV * D, D),
            jnp.broadcast_to(doc_ids.astype(bf16)[:, None], (16, D)),
        ],
        axis=0,
    )[None]

    other_state = swap(state_high)
    half = LOCAL // 2
    half_rate = lax.dynamic_slice_in_dim(decay_rate, core * half, half, 0)
    tile_fade = jnp.exp(-half_rate * TILE)[:, None, None]
    state_mine = lax.dynamic_slice_in_dim(state, core * half, half, 0)
    state_other = lax.dynamic_slice_in_dim(other_state, core * half, half, 0).astype(f32)
    chip_state = jnp.where(core == 0, tile_fade * state_mine + state_other, state_mine + tile_fade * state_other)
    pieces = lax.all_to_all(chip_state.astype(bf16), "zl", 0, 0, tiled=True)

    first_blocks = [chip_shift(block, s) for s in (8, 16, 1, 9)]
    up = jnp.concatenate([first_blocks[2], first_blocks[3]], axis=0)
    down = jnp.concatenate([first_blocks[0], first_blocks[1]], axis=0)
    mate = swap(block)
    qt, *flow = flash(place, doc_ids, block_mask, [mate], [((0,), True)], first=(soft_q, block[0]))

    inner, query = call(
        inner_body, [shape(heads, f32), shape(heads, bf16)], [SMEM, VMEM, VMEM, VMEM], [big] * 3, flops=1 << 28
    )(decay_rate, lin_q, lin_k, lin_v)

    rate = lax.dynamic_slice_in_dim(decay_rate, core * half + 2 * zl, 2, 0)[:, None, None]
    pieces = pieces.reshape(4, 2, D, D).astype(f32)
    chip_fade = jnp.exp(-rate * (2 * TILE))
    row4 = pieces[0]
    prefix = [jnp.zeros_like(row4), row4]
    for k in range(1, 4):
        row4 = row4 * chip_fade + pieces[k]
        prefix.append(row4)
    four_fade = jnp.exp(-rate * (8 * TILE))
    eight_fade = jnp.exp(-rate * (16 * TILE))
    row4_other = swap(row4, "zh")
    row8 = jnp.where(zh == 0, four_fade * row4 + row4_other, row4 + four_fade * row4_other)
    earlier = jnp.zeros_like(row8)
    for k in (3, 2, 1):
        earlier = earlier * eight_fade + jnp.where(x >= k, x_shift(row8, k), 0.0)
    earlier = jnp.where(zh == 1, four_fade * earlier + row4_other, earlier)
    entering = jnp.stack([prefix[k] + jnp.exp(-rate * (2 * TILE * k)) * earlier for k in range(4)])
    near = lax.all_to_all(entering.astype(bf16).reshape(half, D, D), "zl", 0, 0, tiled=True)
    far = swap(near)

    mixed, sums = call(
        outer_body,
        [shape(heads, f32), shape((8, TILE), f32)],
        [SMEM, SMEM] + [VMEM] * 5,
        [pltpu.VMEM((TILE, D), f32)],
        flops=1 << 28,
    )(place, decay_rate, inner, query, near, far, other_state)
    others = [head_shift(sums, s) for s in (1, 2, 3)]

    up_at, down_at = (1, 9), (8, 16)
    for step in range(4):
        groups = [(up_at, False), (down_at, False), (up_at, True), (down_at, True)]
        blocks = [up, down, swap(up), swap(down)]
        done = flash(place, doc_ids, block_mask, blocks, groups, state=(qt, *flow), last=step == 3)
        if step < 3:
            flow = done
            up, down = chip_shift(up, 1), chip_shift(down, -1)
            up_at, down_at = tuple(d + 1 for d in up_at), tuple(d - 1 for d in down_at)

    lin_out = call(norm_body, shape((TILE, LOCAL, D), bf16), [VMEM] * 6, [big])(mixed, sums, *others, norm_gain)
    return lin_out, done


def solution(mesh):
    names = ("x", "zh", "zl", "core", "head")
    fine = Mesh(mesh.devices.reshape(4, 2, 4, 2, 4), names)
    ctx = ("x", "zh", "zl", "core")
    wide = P(ctx, "head", None)
    return jax.shard_map(
        on_device,
        mesh=fine,
        in_specs=(wide, wide, wide, P("head"), P("head", None), wide, wide, wide, P(ctx), P(ctx, None)),
        out_specs=(wide, wide),
        check_vma=False,
    )
```

```python
import functools

import jax
import jax.numpy as jnp
from jax import lax
from jax.experimental import pallas as pl
from jax.experimental.pallas import tpu as pltpu
from jax.sharding import Mesh, PartitionSpec as P

D = 128
TILE = 128
HEADS = 64
LOCAL = 16
KV = 2
GROUPS = 8
ROWS = TILE * GROUPS
BLOCK = 4 * TILE + 16
CHUNK = 512
AHEAD = 2
SCALE = 1.4426950408889634 / D**0.5
LOWEST = -1e30
bf16, f32 = jnp.bfloat16, jnp.float32
CHIPS = ("x", "zh", "zl")
VMEM = pl.BlockSpec(memory_space=pltpu.VMEM)
SMEM = pl.BlockSpec(memory_space=pltpu.SMEM)


def dot(a, b, ca=1, cb=0):
    return lax.dot_general(a, b, (((ca,), (cb,)), ((), ())), preferred_element_type=f32)


def split(value):
    high = value.astype(bf16)
    return high, (value - high.astype(f32)).astype(bf16)


def iota(shape, axis):
    return lax.broadcasted_iota(jnp.int32, shape, axis)


def call(body, outs, ins, scratch=(), flops=0, nbytes=4 << 20):
    return pl.pallas_call(
        body,
        out_shape=outs,
        in_specs=ins,
        out_specs=jax.tree.map(lambda _: VMEM, outs),
        scratch_shapes=list(scratch),
        compiler_params=pltpu.CompilerParams(vmem_limit_bytes=40 << 20),
        cost_estimate=pl.CostEstimate(flops=flops, bytes_accessed=nbytes, transcendentals=0),
    )


def shape(dims, dtype):
    return jax.ShapeDtypeStruct(dims, dtype)


def flash_body(first, last, groups, *refs):
    refs = list(refs)
    place, doc, mask = refs[:3]
    blocks = refs[3 : 3 + len(groups)]
    refs = refs[3 + len(groups) :]
    if first:
        q_in, own = refs[:2]
        refs = refs[2:]
    else:
        qt, peak_in, total_in, acc_in = refs[:4]
        refs = refs[4:]
    if last:
        out = refs[0]
        refs = refs[1:]
        kbuf, vbuf, peak, total, acc = refs
    elif first:
        qt, peak, total, acc, kbuf, vbuf = refs
    else:
        peak, total, acc, kbuf, vbuf = refs

    chip, core = place[0], place[1]
    mine = 2 * chip + core

    def attend(keys, values_t, causal):
        jobs = [(h, c * CHUNK) for h in range(KV) for c in range(ROWS // CHUNK)]

        def score(n):
            h, at = jobs[n]
            return dot(keys[h], qt[h, :, at : at + CHUNK])

        scores = [score(n) for n in range(AHEAD)]
        for n, (h, at) in enumerate(jobs):
            if n + AHEAD < len(jobs):
                scores.append(score(n + AHEAD))
            cols = slice(at, at + CHUNK)
            s = scores[n]
            if causal:
                keep = iota(s.shape, 0) <= (at + iota(s.shape, 1)) // GROUPS
                s = jnp.where(keep, s, LOWEST)
                top = jnp.max(s, axis=0, keepdims=True)
                p = jnp.exp2((s - top) * SCALE)
                total[h, :, cols] = jnp.sum(p, axis=0, keepdims=True)
                acc[h, :, cols] = dot(values_t[h], p.astype(bf16))
            else:
                old = peak[h, :, cols]
                top = jnp.maximum(old, jnp.max(s, axis=0, keepdims=True))
                fade = jnp.exp2((old - top) * SCALE)
                p = jnp.exp2((s - top) * SCALE)
                total[h, :, cols] = total[h, :, cols] * fade + jnp.sum(p, axis=0, keepdims=True)
                acc[h, :, cols] = acc[h, :, cols] * fade + dot(values_t[h], p.astype(bf16))
            peak[h, :, cols] = top

    if first:
        q = q_in[...].astype(f32)
        for h in range(KV):
            qt[h] = q[:, h * GROUPS : (h + 1) * GROUPS, :].reshape(ROWS, D).T.astype(bf16)
        attend([own[h * D : (h + 1) * D] for h in range(KV)], [own[(KV + h) * D : (KV + h + 1) * D] for h in range(KV)], True)
    else:
        peak[...] = peak_in[...]
        total[...] = total_in[...]
        acc[...] = acc_in[...]

    entries = [(r, i) for r in range(len(groups)) for i in range(len(groups[r][0]))]
    docs = jnp.concatenate([blocks[r][i, 4 * D : 4 * D + 16, :].astype(f32)[0:1] for r, i in entries], axis=0)
    weight = jnp.left_shift(1, iota(docs.shape, 0)).astype(f32)
    same = (docs == doc[0].astype(f32)) & (iota(docs.shape, 1) == 0)
    bits = jnp.sum(jnp.where(same, weight, 0.0)).astype(jnp.int32)
    count = jnp.int32(0)
    for n, (r, i) in enumerate(entries):
        dists, swapped = groups[r]
        carrier = 1 - core if swapped else core
        tile = 2 * (chip - jnp.where(carrier == 0, dists[i][0], dists[i][1])) + (carrier if i % 2 == 0 else 1 - carrier)
        ok = (jnp.bitwise_and(lax.shift_right_logical(bits, n), 1) == 1) & (tile >= 0) & (tile < mine)
        ok = ok & (mask[0, jnp.maximum(tile, 0)] == 1)

        @pl.when(ok)
        def _(r=r, i=i, count=count):
            for h in range(KV):
                kbuf[h, count] = blocks[r][i, h * D : (h + 1) * D, :]
                vbuf[h, count] = blocks[r][i, (KV + h) * D : (KV + h + 1) * D, :]

        count = count + ok.astype(jnp.int32)

    def pair(n, carry):
        keys = [jnp.concatenate([kbuf[h, 2 * n], kbuf[h, 2 * n + 1]], axis=0) for h in range(KV)]
        values_t = [jnp.concatenate([vbuf[h, 2 * n], vbuf[h, 2 * n + 1]], axis=1) for h in range(KV)]
        attend(keys, values_t, False)
        return carry

    lax.fori_loop(0, lax.shift_right_logical(count, 1), pair, 0)

    @pl.when(jnp.bitwise_and(count, 1) == 1)
    def _():
        attend([kbuf[h, count - 1] for h in range(KV)], [vbuf[h, count - 1] for h in range(KV)], False)

    if last:
        heads = [(acc[h] / total[h]).T.reshape(TILE, GROUPS, D) for h in range(KV)]
        out[...] = jnp.concatenate(heads, axis=1).astype(bf16)


def flash(place, doc, mask, blocks, groups, first=None, state=None, last=False):
    state_shapes = [shape((KV, 1, ROWS), f32), shape((KV, 1, ROWS), f32), shape((KV, D, ROWS), f32)]
    slots = sum(len(dists) for dists, _ in groups)
    buffers = [pltpu.VMEM((KV, slots, D, D), bf16)] * 2
    if last:
        outs = shape((TILE, LOCAL, D), bf16)
        scratch = buffers + [pltpu.VMEM(s.shape, s.dtype) for s in state_shapes]
    else:
        outs = state_shapes
        scratch = buffers
    if first is not None:
        outs = [shape((KV, D, ROWS), bf16)] + outs
        extra = list(first)
    else:
        extra = list(state)
    body = functools.partial(flash_body, first is not None, last, groups)
    return call(body, outs, [SMEM] * 3 + [VMEM] * (len(blocks) + len(extra)), scratch, flops=slots * (1 << 28))(
        place, doc, mask, *blocks, *extra
    )


def state_body(rate, k_in, v_in, high_out, state_out, kf, vf):
    kf[...] = k_in[...].astype(f32).reshape(TILE * LOCAL, D)
    vf[...] = v_in[...].astype(f32).reshape(TILE * LOCAL, D)
    left = (TILE - iota((TILE, D), 0)).astype(f32)
    for h in range(LOCAL):
        keys = kf[pl.ds(h, TILE, stride=LOCAL), :] * jnp.exp(-rate[h] * left)
        values = vf[pl.ds(h, TILE, stride=LOCAL), :].astype(bf16)
        high, low = split(keys)
        state = dot(high, values, 0, 0) + dot(low, values, 0, 0)
        state_out[h] = state
        high_out[h] = state.astype(bf16)


def inner_body(rate, q_in, k_in, v_in, inner_out, q_out, qf, kf, vf):
    qf[...] = q_in[...].astype(f32).reshape(TILE * LOCAL, D)
    kf[...] = k_in[...].astype(f32).reshape(TILE * LOCAL, D)
    vf[...] = v_in[...].astype(f32).reshape(TILE * LOCAL, D)
    distance = iota((TILE, TILE), 0) - iota((TILE, TILE), 1)
    steps = jnp.maximum(distance, 0).astype(f32)
    for h in range(LOCAL):
        query = qf[pl.ds(h, TILE, stride=LOCAL), :].astype(bf16)
        keys = kf[pl.ds(h, TILE, stride=LOCAL), :].astype(bf16)
        values = vf[pl.ds(h, TILE, stride=LOCAL), :].astype(bf16)
        within = jnp.where(distance >= 0, jnp.exp(-rate[h] * steps), 0.0)
        high, low = split(dot(query, keys, 1, 1) * within)
        inner_out[h] = dot(high, values) + dot(low, values)
        q_out[h] = query


def power(rate, tokens):
    return jnp.exp(jnp.full((1, D), -tokens, f32) * rate)


def chip_body(place, rate, mine, other, *slices):
    core, zl = place[1], place[2]
    first = core == 0
    for s, out in enumerate(slices):
        owner = lax.rem(zl + s, 4)
        for i in range(2):
            h = core * (LOCAL // 2) + 2 * owner + i
            fade = power(rate[h], TILE)
            state, rest = mine[h], other[h].astype(f32)
            out[i] = jnp.where(first, fade * state + rest, state + fade * rest).astype(bf16)


def four_body(place, rate, p0, p1, p2, p3, total, sent):
    core, zl = place[1], place[2]
    for i in range(2):
        r = rate[core * (LOCAL // 2) + 2 * zl + i]
        row = jnp.zeros((D, D), f32)
        for s, piece in enumerate((p0, p1, p2, p3)):
            source = lax.rem(zl + 4 - s, 4)
            row += piece[i].astype(f32) * power(r, ((3 - source) * 2 * TILE).astype(f32))
        total[i] = row
        sent[i] = row.astype(bf16)


def eight_body(place, rate, four, other, out):
    core, zl, zh = place[1], place[2], place[3]
    for i in range(2):
        fade = power(rate[core * (LOCAL // 2) + 2 * zl + i], 8 * TILE)
        mine, rest = four[i], other[i].astype(f32)
        out[i] = jnp.where(zh == 0, fade * mine + rest, mine + fade * rest).astype(bf16)


def entering_body(place, rate, p0, p1, p2, p3, other, x1, x2, x3, *slices):
    core, zl, zh, x = place[1], place[2], place[3], place[4]
    for i in range(2):
        r = rate[core * (LOCAL // 2) + 2 * zl + i]
        earlier = jnp.zeros((D, D), f32)
        for k, part in ((3, x3), (2, x2), (1, x1)):
            earlier = earlier * power(r, 16 * TILE) + jnp.where(x >= k, part[i].astype(f32), 0.0)
        earlier = jnp.where(zh == 1, power(r, 8 * TILE) * earlier + other[i].astype(f32), earlier)
        pieces = [p[i].astype(f32) for p in (p0, p1, p2, p3)]
        for t, out in enumerate(slices):
            target = lax.rem(zl + t, 4)
            state = earlier * power(r, (target * 2 * TILE).astype(f32))
            for s, piece in enumerate(pieces):
                source = lax.rem(zl + 4 - s, 4)
                fade = power(r, (jnp.maximum(target - 1 - source, 0) * 2 * TILE).astype(f32))
                state += jnp.where(source < target, piece * fade, 0.0)
            out[i] = state.astype(bf16)


def outer_body(place, rate, inner, q, near, far, before, mixed_out, sums_out, squares):
    core, zl = place[1], place[2]
    upper = core == 1
    position = iota((TILE, D), 0).astype(f32)
    squares[...] = jnp.zeros_like(squares)
    for half, source in ((core, near), (1 - core, far)):
        for s in range(4):
            owner = lax.rem(zl + 4 - s, 4)
            for i in range(2):
                h = half * (LOCAL // 2) + 2 * owner + i
                r = rate[h]
                entering = source[s, i].astype(f32)
                entering = jnp.where(upper, power(r, TILE) * entering + before[h].astype(f32), entering)
                high, low = split(entering)
                query = q[h]
                outer = (dot(query, high) + dot(query, low)) * jnp.exp(-r * position)
                mixed = inner[h] + outer
                mixed_out[h] = mixed
                squares[...] += mixed * mixed
    sums_out[...] = jnp.broadcast_to(jnp.sum(squares[...].T, axis=0, keepdims=True), (8, TILE))


def norm_body(mixed, own, s1, s2, s3, gain, out, rows):
    sums = own[...] + s1[...] + s2[...] + s3[...]
    inverse = lax.rsqrt(sums / (HEADS * D) + 1e-5)
    inverse = jnp.broadcast_to(inverse[0:1], (D, TILE)).T
    for h in range(LOCAL):
        rows[pl.ds(h, TILE, stride=LOCAL), :] = mixed[h] * inverse * gain[h : h + 1, :]
    out[...] = rows[...].reshape(TILE, LOCAL, D).astype(bf16)


def two_ways(value, steps0, steps1):
    pairs = [(2 * i + c, 2 * ((i + s) % 32) + c) for i in range(32) for c, s in ((0, steps0), (1, steps1))]
    return lax.ppermute(value, (*CHIPS, "core"), pairs)


def x_shift(value, steps):
    return lax.ppermute(value, "x", [(i, (i + steps) % 4) for i in range(4)])


def head_shift(value, steps):
    return lax.ppermute(value, "head", [(i, (i + steps) % 4) for i in range(4)])


def zl_shift(value, steps):
    return lax.ppermute(value, "zl", [(i, (i + steps) % 4) for i in range(4)])


def swap(value, axis="core"):
    return lax.ppermute(value, axis, [(0, 1), (1, 0)])


def after(value, *others):
    return lax.optimization_barrier((value, *others))[0]


def on_device(lin_q, lin_k, lin_v, decay_rate, norm_gain, soft_q, soft_k, soft_v, doc_ids, block_mask):
    x, zh, zl, core = (lax.axis_index(a) for a in ("x", "zh", "zl", "core"))
    chip = (x * 2 + zh) * 4 + zl
    place = jnp.stack([chip, core, zl, zh, x]).astype(jnp.int32)
    big = pltpu.VMEM((TILE * LOCAL, D), f32)
    heads = (LOCAL, D, D)
    pair = (2, D, D)

    block = jnp.concatenate(
        [
            jnp.transpose(soft_k, (1, 0, 2)).reshape(KV * D, D),
            jnp.transpose(soft_v, (1, 2, 0)).reshape(KV * D, D),
            jnp.broadcast_to(doc_ids.astype(bf16)[:, None], (16, D)),
        ],
        axis=0,
    )[None]
    mate = swap(block)
    both = jnp.concatenate((block, mate), axis=0)
    arrived = two_ways(both, 1, 8), two_ways(both, 9, 16)

    state_high, state = call(
        state_body, [shape(heads, bf16), shape(heads, f32)], [SMEM, VMEM, VMEM], [big, big], flops=1 << 30
    )(decay_rate, after(lin_k, both), lin_v)
    other_state = swap(state_high)
    slices = call(chip_body, [shape(pair, bf16)] * 4, [SMEM, SMEM, VMEM, VMEM])(place, decay_rate, state, other_state)
    pieces = [slices[0]] + [zl_shift(slices[k], k) for k in (1, 2, 3)]

    inner, query = call(
        inner_body, [shape(heads, f32), shape(heads, bf16)], [SMEM, VMEM, VMEM, VMEM], [big] * 3, flops=1 << 30
    )(decay_rate, after(lin_q, slices[0]), lin_k, lin_v)

    row4, row4_sent = call(four_body, [shape(pair, f32), shape(pair, bf16)], [SMEM, SMEM] + [VMEM] * 4)(
        place, decay_rate, *pieces
    )
    row4_other = swap(row4_sent, "zh")

    def attend(blocks, groups, **state):
        return flash(place, doc_ids, block_mask, blocks, groups, **state)

    def parts(k):
        dists = ((1 + k, 8 - k),) * 2 + ((9 + k, 16 - k),) * 2
        return [carried, swap(carried)], [(dists, False), (dists, True)]

    qt, *flow = attend([mate], [(((0, 0),), True)], first=(after(soft_q, row4_sent), block[0]))
    row4 = after(row4, flow[0])
    carried = after(jnp.concatenate(after(arrived, query, row4_sent), axis=0), row4_other, flow[0])
    chips0 = parts(0)
    carried = two_ways(carried, 1, -1)

    row8 = call(eight_body, shape(pair, bf16), [SMEM, SMEM, VMEM, VMEM])(place, decay_rate, row4, row4_other)
    earlier = [x_shift(row8, k) for k in (1, 2, 3)]
    flow = attend(*chips0, state=(qt, *after(tuple(flow), row8)))
    earlier = after(tuple(earlier), flow[0])
    carried = after(carried, *earlier)
    chips1 = parts(1)
    carried = two_ways(carried, 1, -1)

    entering = call(entering_body, [shape(pair, bf16)] * 4, [SMEM, SMEM] + [VMEM] * 8)(
        place, decay_rate, *pieces, row4_other, *earlier
    )
    near = jnp.stack([entering[0]] + [zl_shift(entering[k], k) for k in (1, 2, 3)])
    flow = attend(*chips1, state=(qt, *after(tuple(flow), entering[0])))
    near = after(near, flow[0])
    carried = after(carried, flow[0])
    chips2 = parts(2)
    carried = two_ways(carried, 1, -1)

    far = swap(near)
    mixed, sums = call(
        outer_body,
        [shape(heads, f32), shape((8, TILE), f32)],
        [SMEM, SMEM] + [VMEM] * 5,
        [pltpu.VMEM((TILE, D), f32)],
        flops=1 << 30,
    )(place, decay_rate, inner, query, near, far, other_state)
    others = [head_shift(sums, s) for s in (1, 2, 3)]
    flow = attend(*chips2, state=(qt, *after(tuple(flow), sums)))
    carried, *flow = after((carried, *flow), *others)
    soft_out = attend(*parts(3), state=(qt, *flow), last=True)
    lin_out = call(norm_body, shape((TILE, LOCAL, D), bf16), [VMEM] * 6, [big])(
        after(mixed, soft_out), sums, *others, norm_gain
    )
    return lin_out, soft_out


def solution(mesh):
    names = ("x", "zh", "zl", "core", "head")
    fine = Mesh(mesh.devices.reshape(4, 2, 4, 2, 4), names)
    ctx = ("x", "zh", "zl", "core")
    wide = P(ctx, "head", None)
    return jax.shard_map(
        on_device,
        mesh=fine,
        in_specs=(wide, wide, wide, P("head"), P("head", None), wide, wide, wide, P(ctx), P(ctx, None)),
        out_specs=(wide, wide),
        check_vma=False,
    )
```

```python
import functools

import jax
import jax.numpy as jnp
from jax import lax
from jax.experimental import pallas as pl
from jax.experimental.pallas import tpu as pltpu
from jax.sharding import Mesh, PartitionSpec as P

D = 128
TILE = 128
HEADS = 64
LOCAL = 16
KV = 2
GROUPS = 8
ROWS = TILE * GROUPS
BLOCK = 4 * TILE + 16
CHUNK = 512
AHEAD = 2
SCALE = 1.4426950408889634 / D**0.5
LOWEST = -1e30
bf16, f32 = jnp.bfloat16, jnp.float32
CHIPS = ("x", "zh", "zl")
VMEM = pl.BlockSpec(memory_space=pltpu.VMEM)
SMEM = pl.BlockSpec(memory_space=pltpu.SMEM)


def dot(a, b, ca=1, cb=0):
    return lax.dot_general(a, b, (((ca,), (cb,)), ((), ())), preferred_element_type=f32)


def split(value):
    high = value.astype(bf16)
    return high, (value - high.astype(f32)).astype(bf16)


def iota(shape, axis):
    return lax.broadcasted_iota(jnp.int32, shape, axis)


def call(body, outs, ins, scratch=(), flops=0, nbytes=4 << 20):
    return pl.pallas_call(
        body,
        out_shape=outs,
        in_specs=ins,
        out_specs=jax.tree.map(lambda _: VMEM, outs),
        scratch_shapes=list(scratch),
        compiler_params=pltpu.CompilerParams(vmem_limit_bytes=40 << 20),
        cost_estimate=pl.CostEstimate(flops=flops, bytes_accessed=nbytes, transcendentals=0),
    )


def shape(dims, dtype):
    return jax.ShapeDtypeStruct(dims, dtype)


def flash_body(first, last, groups, *refs):
    refs = list(refs)
    place, doc, mask = refs[:3]
    blocks = refs[3 : 3 + len(groups)]
    refs = refs[3 + len(groups) :]
    if first:
        q_in, own = refs[:2]
        refs = refs[2:]
    else:
        qt, peak_in, total_in, acc_in = refs[:4]
        refs = refs[4:]
    if last:
        out = refs[0]
        refs = refs[1:]
        kbuf, vbuf, peak, total, acc = refs
    elif first:
        qt, peak, total, acc, kbuf, vbuf = refs
    else:
        peak, total, acc, kbuf, vbuf = refs

    chip, core = place[0], place[1]
    mine = 2 * chip + core

    def attend(keys, values_t, causal):
        jobs = [(h, c * CHUNK) for h in range(KV) for c in range(ROWS // CHUNK)]

        def score(n):
            h, at = jobs[n]
            return dot(keys[h], qt[h, :, at : at + CHUNK])

        scores = [score(n) for n in range(AHEAD)]
        for n, (h, at) in enumerate(jobs):
            if n + AHEAD < len(jobs):
                scores.append(score(n + AHEAD))
            cols = slice(at, at + CHUNK)
            s = scores[n]
            if causal:
                keep = iota(s.shape, 0) <= (at + iota(s.shape, 1)) // GROUPS
                s = jnp.where(keep, s, LOWEST)
                top = jnp.max(s, axis=0, keepdims=True)
                p = jnp.exp2((s - top) * SCALE)
                total[h, :, cols] = jnp.sum(p, axis=0, keepdims=True)
                acc[h, :, cols] = dot(values_t[h], p.astype(bf16))
            else:
                old = peak[h, :, cols]
                top = jnp.maximum(old, jnp.max(s, axis=0, keepdims=True))
                fade = jnp.exp2((old - top) * SCALE)
                p = jnp.exp2((s - top) * SCALE)
                total[h, :, cols] = total[h, :, cols] * fade + jnp.sum(p, axis=0, keepdims=True)
                acc[h, :, cols] = acc[h, :, cols] * fade + dot(values_t[h], p.astype(bf16))
            peak[h, :, cols] = top

    if first:
        q = q_in[...].astype(f32)
        for h in range(KV):
            qt[h] = q[:, h * GROUPS : (h + 1) * GROUPS, :].reshape(ROWS, D).T.astype(bf16)
        attend([own[h * D : (h + 1) * D] for h in range(KV)], [own[(KV + h) * D : (KV + h + 1) * D] for h in range(KV)], True)
    else:
        peak[...] = peak_in[...]
        total[...] = total_in[...]
        acc[...] = acc_in[...]

    entries = [(r, i) for r in range(len(groups)) for i in range(len(groups[r][0]))]
    docs = jnp.concatenate([blocks[r][i, 4 * D : 4 * D + 16, :].astype(f32)[0:1] for r, i in entries], axis=0)
    weight = jnp.left_shift(1, iota(docs.shape, 0)).astype(f32)
    same = (docs == doc[0].astype(f32)) & (iota(docs.shape, 1) == 0)
    bits = jnp.sum(jnp.where(same, weight, 0.0)).astype(jnp.int32)
    count = jnp.int32(0)
    for n, (r, i) in enumerate(entries):
        dists, swapped = groups[r]
        carrier = 1 - core if swapped else core
        tile = 2 * (chip - jnp.where(carrier == 0, dists[i][0], dists[i][1])) + (carrier if i % 2 == 0 else 1 - carrier)
        ok = (jnp.bitwise_and(lax.shift_right_logical(bits, n), 1) == 1) & (tile >= 0) & (tile < mine)
        ok = ok & (mask[0, jnp.maximum(tile, 0)] == 1)

        @pl.when(ok)
        def _(r=r, i=i, count=count):
            for h in range(KV):
                kbuf[h, count] = blocks[r][i, h * D : (h + 1) * D, :]
                vbuf[h, count] = blocks[r][i, (KV + h) * D : (KV + h + 1) * D, :]

        count = count + ok.astype(jnp.int32)

    def pair(n, carry):
        keys = [jnp.concatenate([kbuf[h, 2 * n], kbuf[h, 2 * n + 1]], axis=0) for h in range(KV)]
        values_t = [jnp.concatenate([vbuf[h, 2 * n], vbuf[h, 2 * n + 1]], axis=1) for h in range(KV)]
        attend(keys, values_t, False)
        return carry

    lax.fori_loop(0, lax.shift_right_logical(count, 1), pair, 0)

    @pl.when(jnp.bitwise_and(count, 1) == 1)
    def _():
        attend([kbuf[h, count - 1] for h in range(KV)], [vbuf[h, count - 1] for h in range(KV)], False)

    if last:
        heads = [(acc[h] / total[h]).T.reshape(TILE, GROUPS, D) for h in range(KV)]
        out[...] = jnp.concatenate(heads, axis=1).astype(bf16)


def flash(place, doc, mask, blocks, groups, first=None, state=None, last=False):
    state_shapes = [shape((KV, 1, ROWS), f32), shape((KV, 1, ROWS), f32), shape((KV, D, ROWS), f32)]
    slots = sum(len(dists) for dists, _ in groups)
    buffers = [pltpu.VMEM((KV, slots, D, D), bf16)] * 2
    if last:
        outs = shape((TILE, LOCAL, D), bf16)
        scratch = buffers + [pltpu.VMEM(s.shape, s.dtype) for s in state_shapes]
    else:
        outs = state_shapes
        scratch = buffers
    if first is not None:
        outs = [shape((KV, D, ROWS), bf16)] + outs
        extra = list(first)
    else:
        extra = list(state)
    body = functools.partial(flash_body, first is not None, last, groups)
    return call(body, outs, [SMEM] * 3 + [VMEM] * (len(blocks) + len(extra)), scratch, flops=slots * (1 << 28))(
        place, doc, mask, *blocks, *extra
    )


def state_body(rate, k_in, v_in, high_out, state_out, kf, vf):
    kf[...] = k_in[...].astype(f32).reshape(TILE * LOCAL, D)
    vf[...] = v_in[...].astype(f32).reshape(TILE * LOCAL, D)
    left = (TILE - iota((TILE, D), 0)).astype(f32)
    for h in range(LOCAL):
        keys = kf[pl.ds(h, TILE, stride=LOCAL), :] * jnp.exp(-rate[h] * left)
        values = vf[pl.ds(h, TILE, stride=LOCAL), :].astype(bf16)
        high, low = split(keys)
        state = dot(high, values, 0, 0) + dot(low, values, 0, 0)
        state_out[h] = state
        high_out[h] = state.astype(bf16)


def inner_body(rate, q_in, k_in, v_in, inner_out, q_out, qf, kf, vf):
    qf[...] = q_in[...].astype(f32).reshape(TILE * LOCAL, D)
    kf[...] = k_in[...].astype(f32).reshape(TILE * LOCAL, D)
    vf[...] = v_in[...].astype(f32).reshape(TILE * LOCAL, D)
    distance = iota((TILE, TILE), 0) - iota((TILE, TILE), 1)
    steps = jnp.maximum(distance, 0).astype(f32)
    for h in range(LOCAL):
        query = qf[pl.ds(h, TILE, stride=LOCAL), :].astype(bf16)
        keys = kf[pl.ds(h, TILE, stride=LOCAL), :].astype(bf16)
        values = vf[pl.ds(h, TILE, stride=LOCAL), :].astype(bf16)
        within = jnp.where(distance >= 0, jnp.exp(-rate[h] * steps), 0.0)
        high, low = split(dot(query, keys, 1, 1) * within)
        inner_out[h] = dot(high, values) + dot(low, values)
        q_out[h] = query


def power(rate, tokens):
    return jnp.exp(jnp.full((1, D), -tokens, f32) * rate)


def chip_body(place, rate, mine, other, *slices):
    core, zl = place[1], place[2]
    first = core == 0
    for s, out in enumerate(slices):
        owner = jnp.bitwise_xor(zl, s)
        for i in range(2):
            h = core * (LOCAL // 2) + 2 * owner + i
            fade = power(rate[h], TILE)
            state, rest = mine[h], other[h].astype(f32)
            out[i] = jnp.where(first, fade * state + rest, state + fade * rest).astype(bf16)


def four_body(place, rate, p0, p1, p2, p3, total, sent):
    core, zl = place[1], place[2]
    for i in range(2):
        r = rate[core * (LOCAL // 2) + 2 * zl + i]
        row = jnp.zeros((D, D), f32)
        for s, piece in enumerate((p0, p1, p2, p3)):
            source = jnp.bitwise_xor(zl, s)
            row += piece[i].astype(f32) * power(r, ((3 - source) * 2 * TILE).astype(f32))
        total[i] = row
        sent[i] = row.astype(bf16)


def row_body(place, rate, four, x1, x2, x3, own, out):
    core, zl, zh, x = place[1], place[2], place[3], place[4]
    for i in range(2):
        r = rate[core * (LOCAL // 2) + 2 * zl + i]
        earlier = jnp.zeros((D, D), f32)
        for k, part in ((1, x1), (2, x2), (3, x3)):
            source = jnp.bitwise_xor(x, k)
            fade = power(r, (jnp.maximum(x - 1 - source, 0) * 16 * TILE).astype(f32))
            earlier += jnp.where(source < x, part[i].astype(f32) * fade, 0.0)
        own[i] = power(r, 8 * TILE) * earlier
        out[i] = jnp.where(zh == 0, power(r, 16 * TILE) * earlier + four[i], earlier).astype(bf16)


def entering_body(place, rate, p0, p1, p2, p3, own, other, *slices):
    core, zl = place[1], place[2]
    for i in range(2):
        r = rate[core * (LOCAL // 2) + 2 * zl + i]
        earlier = own[i] + other[i].astype(f32)
        pieces = [p[i].astype(f32) for p in (p0, p1, p2, p3)]
        for t, out in enumerate(slices):
            target = jnp.bitwise_xor(zl, t)
            state = earlier * power(r, (target * 2 * TILE).astype(f32))
            for s, piece in enumerate(pieces):
                source = jnp.bitwise_xor(zl, s)
                fade = power(r, (jnp.maximum(target - 1 - source, 0) * 2 * TILE).astype(f32))
                state += jnp.where(source < target, piece * fade, 0.0)
            out[i] = state.astype(bf16)


def outer_body(place, rate, inner, q, near, far, before, mixed_out, sums_out, squares):
    core, zl = place[1], place[2]
    upper = core == 1
    position = iota((TILE, D), 0).astype(f32)
    squares[...] = jnp.zeros_like(squares)
    for half, source in ((core, near), (1 - core, far)):
        for s in range(4):
            owner = jnp.bitwise_xor(zl, s)
            for i in range(2):
                h = half * (LOCAL // 2) + 2 * owner + i
                r = rate[h]
                entering = source[s, i].astype(f32)
                entering = jnp.where(upper, power(r, TILE) * entering + before[h].astype(f32), entering)
                high, low = split(entering)
                query = q[h]
                outer = (dot(query, high) + dot(query, low)) * jnp.exp(-r * position)
                mixed = inner[h] + outer
                mixed_out[h] = mixed
                squares[...] += mixed * mixed
    sums_out[...] = jnp.broadcast_to(jnp.sum(squares[...].T, axis=0, keepdims=True), (8, TILE))


def norm_body(mixed, own, s1, s2, s3, gain, out, rows):
    sums = own[...] + s1[...] + s2[...] + s3[...]
    inverse = lax.rsqrt(sums / (HEADS * D) + 1e-5)
    inverse = jnp.broadcast_to(inverse[0:1], (D, TILE)).T
    for h in range(LOCAL):
        rows[pl.ds(h, TILE, stride=LOCAL), :] = mixed[h] * inverse * gain[h : h + 1, :]
    out[...] = rows[...].reshape(TILE, LOCAL, D).astype(bf16)


def two_ways(value, steps0, steps1):
    pairs = [(2 * i + c, 2 * ((i + s) % 32) + c) for i in range(32) for c, s in ((0, steps0), (1, steps1))]
    return lax.ppermute(value, (*CHIPS, "core"), pairs)


def trade(value, axis, bits):
    return lax.ppermute(value, axis, [(i, i ^ bits) for i in range(4)])


def swap(value, axis="core"):
    return lax.ppermute(value, axis, [(0, 1), (1, 0)])


def after(value, *others):
    return lax.optimization_barrier((value, *others))[0]


def on_device(lin_q, lin_k, lin_v, decay_rate, norm_gain, soft_q, soft_k, soft_v, doc_ids, block_mask):
    x, zh, zl, core = (lax.axis_index(a) for a in ("x", "zh", "zl", "core"))
    chip = (x * 2 + zh) * 4 + zl
    place = jnp.stack([chip, core, zl, zh, x]).astype(jnp.int32)
    big = pltpu.VMEM((TILE * LOCAL, D), f32)
    heads = (LOCAL, D, D)
    pair = (2, D, D)

    block = jnp.concatenate(
        [
            jnp.transpose(soft_k, (1, 0, 2)).reshape(KV * D, D),
            jnp.transpose(soft_v, (1, 2, 0)).reshape(KV * D, D),
            jnp.broadcast_to(doc_ids.astype(bf16)[:, None], (16, D)),
        ],
        axis=0,
    )[None]
    mate = swap(block)
    both = jnp.concatenate((block, mate), axis=0)
    arrived = two_ways(both, 1, 8), two_ways(both, 9, 16)

    state_high, state = call(
        state_body, [shape(heads, bf16), shape(heads, f32)], [SMEM, VMEM, VMEM], [big, big], flops=1 << 30
    )(decay_rate, after(lin_k, both), lin_v)
    other_state = swap(state_high)
    slices = call(chip_body, [shape(pair, bf16)] * 4, [SMEM, SMEM, VMEM, VMEM])(place, decay_rate, state, other_state)
    pieces = [slices[0]] + [trade(slices[k], "zl", k) for k in (1, 2, 3)]

    inner, query = call(
        inner_body, [shape(heads, f32), shape(heads, bf16)], [SMEM, VMEM, VMEM, VMEM], [big] * 3, flops=1 << 30
    )(decay_rate, after(lin_q, slices[0]), lin_k, lin_v)

    row4, row4_sent = call(four_body, [shape(pair, f32), shape(pair, bf16)], [SMEM, SMEM] + [VMEM] * 4)(
        place, decay_rate, *pieces
    )
    earlier = [trade(row4_sent, "x", k) for k in (1, 2, 3)]

    def attend(blocks, groups, **state):
        return flash(place, doc_ids, block_mask, blocks, groups, **state)

    def parts(k):
        dists = ((1 + k, 8 - k),) * 2 + ((9 + k, 16 - k),) * 2
        return [carried, swap(carried)], [(dists, False), (dists, True)]

    qt, *flow = attend([mate], [(((0, 0),), True)], first=(after(soft_q, row4_sent), block[0]))
    row4 = after(row4, flow[0])
    carried = after(jnp.concatenate(after(arrived, query, row4_sent), axis=0), flow[0], *earlier)
    chips0 = parts(0)
    carried = two_ways(carried, 1, -1)

    row_own, row_sent = call(row_body, [shape(pair, f32), shape(pair, bf16)], [SMEM, SMEM] + [VMEM] * 4)(
        place, decay_rate, row4, *earlier
    )
    row_other = swap(row_sent, "zh")
    flow = attend(*chips0, state=(qt, *after(tuple(flow), row_sent)))
    row_other = after(row_other, flow[0])
    carried = after(carried, row_other)
    chips1 = parts(1)
    carried = two_ways(carried, 1, -1)

    entering = call(entering_body, [shape(pair, bf16)] * 4, [SMEM, SMEM] + [VMEM] * 6)(
        place, decay_rate, *pieces, row_own, row_other
    )
    near = jnp.stack([entering[0]] + [trade(entering[k], "zl", k) for k in (1, 2, 3)])
    flow = attend(*chips1, state=(qt, *after(tuple(flow), entering[0])))
    near = after(near, flow[0])
    carried = after(carried, flow[0])
    chips2 = parts(2)
    carried = two_ways(carried, 1, -1)

    far = swap(near)
    mixed, sums = call(
        outer_body,
        [shape(heads, f32), shape((8, TILE), f32)],
        [SMEM, SMEM] + [VMEM] * 5,
        [pltpu.VMEM((TILE, D), f32)],
        flops=1 << 30,
    )(place, decay_rate, inner, query, near, far, other_state)
    others = [trade(sums, "head", s) for s in (1, 2, 3)]
    flow = attend(*chips2, state=(qt, *after(tuple(flow), sums)))
    carried, *flow = after((carried, *flow), *others)
    (local, swapped), (local_at, swapped_at) = parts(3)
    flow = attend([local], [local_at], state=(qt, *flow))
    soft_out = attend([swapped], [swapped_at], state=(qt, *flow), last=True)
    lin_out = call(norm_body, shape((TILE, LOCAL, D), bf16), [VMEM] * 6, [big])(
        after(mixed, soft_out), sums, *others, norm_gain
    )
    return lin_out, soft_out


def solution(mesh):
    names = ("x", "zh", "zl", "core", "head")
    fine = Mesh(mesh.devices.reshape(4, 2, 4, 2, 4), names)
    ctx = ("x", "zh", "zl", "core")
    wide = P(ctx, "head", None)
    return jax.shard_map(
        on_device,
        mesh=fine,
        in_specs=(wide, wide, wide, P("head"), P("head", None), wide, wide, wide, P(ctx), P(ctx, None)),
        out_specs=(wide, wide),
        check_vma=False,
    )
```

```python
import functools

import jax
import jax.numpy as jnp
from jax import lax
from jax.experimental import pallas as pl
from jax.experimental.pallas import tpu as pltpu
from jax.sharding import Mesh, PartitionSpec as P

D = 128
TILE = 128
HEADS = 64
LOCAL = 16
KV = 2
GROUPS = 8
ROWS = TILE * GROUPS
BLOCK = 4 * TILE + 16
CHUNK = 512
AHEAD = 2
SCALE = 1.4426950408889634 / D**0.5
LOWEST = -1e30
bf16, f32 = jnp.bfloat16, jnp.float32
CHIPS = ("x", "zh", "zl")
VMEM = pl.BlockSpec(memory_space=pltpu.VMEM)
SMEM = pl.BlockSpec(memory_space=pltpu.SMEM)


def dot(a, b, ca=1, cb=0):
    return lax.dot_general(a, b, (((ca,), (cb,)), ((), ())), preferred_element_type=f32)


def split(value):
    high = value.astype(bf16)
    return high, (value - high.astype(f32)).astype(bf16)


def iota(shape, axis):
    return lax.broadcasted_iota(jnp.int32, shape, axis)


def call(body, outs, ins, scratch=(), flops=0, nbytes=4 << 20):
    return pl.pallas_call(
        body,
        out_shape=outs,
        in_specs=ins,
        out_specs=jax.tree.map(lambda _: VMEM, outs),
        scratch_shapes=list(scratch),
        compiler_params=pltpu.CompilerParams(vmem_limit_bytes=40 << 20),
        cost_estimate=pl.CostEstimate(flops=flops, bytes_accessed=nbytes, transcendentals=0),
    )


def shape(dims, dtype):
    return jax.ShapeDtypeStruct(dims, dtype)


def flash_body(first, last, groups, *refs):
    refs = list(refs)
    place, doc, mask = refs[:3]
    blocks = refs[3 : 3 + len(groups)]
    refs = refs[3 + len(groups) :]
    if first:
        q_in, own = refs[:2]
        refs = refs[2:]
    else:
        qt, peak_in, total_in, acc_in = refs[:4]
        refs = refs[4:]
    if last:
        out = refs[0]
        refs = refs[1:]
        kbuf, vbuf, peak, total, acc = refs
    elif first:
        qt, peak, total, acc, kbuf, vbuf = refs
    else:
        peak, total, acc, kbuf, vbuf = refs

    chip, core = place[0], place[1]
    mine = 2 * chip + core

    def attend(keys, values_t, causal):
        jobs = [(h, c * CHUNK) for h in range(KV) for c in range(ROWS // CHUNK)]

        def score(n):
            h, at = jobs[n]
            return dot(keys[h], qt[h, :, at : at + CHUNK])

        scores = [score(n) for n in range(AHEAD)]
        for n, (h, at) in enumerate(jobs):
            if n + AHEAD < len(jobs):
                scores.append(score(n + AHEAD))
            cols = slice(at, at + CHUNK)
            s = scores[n]
            if causal:
                keep = iota(s.shape, 0) <= (at + iota(s.shape, 1)) // GROUPS
                s = jnp.where(keep, s, LOWEST)
                top = jnp.max(s, axis=0, keepdims=True)
                p = jnp.exp2((s - top) * SCALE)
                total[h, :, cols] = jnp.sum(p, axis=0, keepdims=True)
                acc[h, :, cols] = dot(values_t[h], p.astype(bf16))
            else:
                old = peak[h, :, cols]
                top = jnp.maximum(old, jnp.max(s, axis=0, keepdims=True))
                fade = jnp.exp2((old - top) * SCALE)
                p = jnp.exp2((s - top) * SCALE)
                total[h, :, cols] = total[h, :, cols] * fade + jnp.sum(p, axis=0, keepdims=True)
                acc[h, :, cols] = acc[h, :, cols] * fade + dot(values_t[h], p.astype(bf16))
            peak[h, :, cols] = top

    if first:
        q = q_in[...].astype(f32)
        for h in range(KV):
            qt[h] = q[:, h * GROUPS : (h + 1) * GROUPS, :].reshape(ROWS, D).T.astype(bf16)
        attend([own[h * D : (h + 1) * D] for h in range(KV)], [own[(KV + h) * D : (KV + h + 1) * D] for h in range(KV)], True)
    else:
        peak[...] = peak_in[...]
        total[...] = total_in[...]
        acc[...] = acc_in[...]

    entries = [(r, i) for r in range(len(groups)) for i in range(len(groups[r][0]))]
    docs = jnp.concatenate([blocks[r][i, 4 * D : 4 * D + 16, :].astype(f32)[0:1] for r, i in entries], axis=0)
    weight = jnp.left_shift(1, iota(docs.shape, 0)).astype(f32)
    same = (docs == doc[0].astype(f32)) & (iota(docs.shape, 1) == 0)
    bits = jnp.sum(jnp.where(same, weight, 0.0)).astype(jnp.int32)
    count = jnp.int32(0)
    for n, (r, i) in enumerate(entries):
        dists, swapped = groups[r]
        carrier = 1 - core if swapped else core
        tile = 2 * (chip - jnp.where(carrier == 0, dists[i][0], dists[i][1])) + (carrier if i % 2 == 0 else 1 - carrier)
        ok = (jnp.bitwise_and(lax.shift_right_logical(bits, n), 1) == 1) & (tile >= 0) & (tile < mine)
        ok = ok & (mask[0, jnp.maximum(tile, 0)] == 1)

        @pl.when(ok)
        def _(r=r, i=i, count=count):
            for h in range(KV):
                kbuf[h, count] = blocks[r][i, h * D : (h + 1) * D, :]
                vbuf[h, count] = blocks[r][i, (KV + h) * D : (KV + h + 1) * D, :]

        count = count + ok.astype(jnp.int32)

    def pair(n, carry):
        keys = [jnp.concatenate([kbuf[h, 2 * n], kbuf[h, 2 * n + 1]], axis=0) for h in range(KV)]
        values_t = [jnp.concatenate([vbuf[h, 2 * n], vbuf[h, 2 * n + 1]], axis=1) for h in range(KV)]
        attend(keys, values_t, False)
        return carry

    lax.fori_loop(0, lax.shift_right_logical(count, 1), pair, 0)

    @pl.when(jnp.bitwise_and(count, 1) == 1)
    def _():
        attend([kbuf[h, count - 1] for h in range(KV)], [vbuf[h, count - 1] for h in range(KV)], False)

    if last:
        heads = [(acc[h] / total[h]).T.reshape(TILE, GROUPS, D) for h in range(KV)]
        out[...] = jnp.concatenate(heads, axis=1).astype(bf16)


def flash(place, doc, mask, blocks, groups, first=None, state=None, last=False):
    state_shapes = [shape((KV, 1, ROWS), f32), shape((KV, 1, ROWS), f32), shape((KV, D, ROWS), f32)]
    slots = sum(len(dists) for dists, _ in groups)
    buffers = [pltpu.VMEM((KV, slots, D, D), bf16)] * 2
    if last:
        outs = shape((TILE, LOCAL, D), bf16)
        scratch = buffers + [pltpu.VMEM(s.shape, s.dtype) for s in state_shapes]
    else:
        outs = state_shapes
        scratch = buffers
    if first is not None:
        outs = [shape((KV, D, ROWS), bf16)] + outs
        extra = list(first)
    else:
        extra = list(state)
    body = functools.partial(flash_body, first is not None, last, groups)
    return call(body, outs, [SMEM] * 3 + [VMEM] * (len(blocks) + len(extra)), scratch, flops=slots * (1 << 28))(
        place, doc, mask, *blocks, *extra
    )


def state_body(rate, k_in, v_in, high_out, state_out, kf, vf):
    kf[...] = k_in[...].astype(f32).reshape(TILE * LOCAL, D)
    vf[...] = v_in[...].astype(f32).reshape(TILE * LOCAL, D)
    left = (TILE - iota((TILE, D), 0)).astype(f32)
    for h in range(LOCAL):
        keys = kf[pl.ds(h, TILE, stride=LOCAL), :] * jnp.exp(-rate[h] * left)
        values = vf[pl.ds(h, TILE, stride=LOCAL), :].astype(bf16)
        high, low = split(keys)
        state = dot(high, values, 0, 0) + dot(low, values, 0, 0)
        state_out[h] = state
        high_out[h] = state.astype(bf16)


def inner_body(rate, q_in, k_in, v_in, inner_out, q_out, qf, kf, vf):
    qf[...] = q_in[...].astype(f32).reshape(TILE * LOCAL, D)
    kf[...] = k_in[...].astype(f32).reshape(TILE * LOCAL, D)
    vf[...] = v_in[...].astype(f32).reshape(TILE * LOCAL, D)
    distance = iota((TILE, TILE), 0) - iota((TILE, TILE), 1)
    steps = jnp.maximum(distance, 0).astype(f32)
    for h in range(LOCAL):
        query = qf[pl.ds(h, TILE, stride=LOCAL), :].astype(bf16)
        keys = kf[pl.ds(h, TILE, stride=LOCAL), :].astype(bf16)
        values = vf[pl.ds(h, TILE, stride=LOCAL), :].astype(bf16)
        within = jnp.where(distance >= 0, jnp.exp(-rate[h] * steps), 0.0)
        high, low = split(dot(query, keys, 1, 1) * within)
        inner_out[h] = dot(high, values) + dot(low, values)
        q_out[h] = query


def power(rate, tokens):
    return jnp.exp(jnp.full((1, D), -tokens, f32) * rate)


def chip_body(place, rate, mine, other, *slices):
    core, zl = place[1], place[2]
    first = core == 0
    for s, out in enumerate(slices):
        owner = jnp.bitwise_xor(zl, s)
        for i in range(2):
            h = core * (LOCAL // 2) + 2 * owner + i
            fade = power(rate[h], TILE)
            state, rest = mine[h], other[h].astype(f32)
            out[i] = jnp.where(first, fade * state + rest, state + fade * rest).astype(bf16)


def four_body(place, rate, p0, p1, p2, p3, total, sent):
    core, zl = place[1], place[2]
    for i in range(2):
        r = rate[core * (LOCAL // 2) + 2 * zl + i]
        row = jnp.zeros((D, D), f32)
        for s, piece in enumerate((p0, p1, p2, p3)):
            source = jnp.bitwise_xor(zl, s)
            row += piece[i].astype(f32) * power(r, ((3 - source) * 2 * TILE).astype(f32))
        total[i] = row
        sent[i] = row.astype(bf16)


def row_body(place, rate, four, x1, x2, x3, own, out):
    core, zl, zh, x = place[1], place[2], place[3], place[4]
    for i in range(2):
        r = rate[core * (LOCAL // 2) + 2 * zl + i]
        earlier = jnp.zeros((D, D), f32)
        for k, part in ((1, x1), (2, x2), (3, x3)):
            source = jnp.bitwise_xor(x, k)
            fade = power(r, (jnp.maximum(x - 1 - source, 0) * 16 * TILE).astype(f32))
            earlier += jnp.where(source < x, part[i].astype(f32) * fade, 0.0)
        own[i] = power(r, 8 * TILE) * earlier
        out[i] = jnp.where(zh == 0, power(r, 16 * TILE) * earlier + four[i], earlier).astype(bf16)


def entering_body(place, rate, p0, p1, p2, p3, own, other, *slices):
    core, zl = place[1], place[2]
    for i in range(2):
        r = rate[core * (LOCAL // 2) + 2 * zl + i]
        earlier = own[i] + other[i].astype(f32)
        pieces = [p[i].astype(f32) for p in (p0, p1, p2, p3)]
        for t, out in enumerate(slices):
            target = jnp.bitwise_xor(zl, t)
            state = earlier * power(r, (target * 2 * TILE).astype(f32))
            for s, piece in enumerate(pieces):
                source = jnp.bitwise_xor(zl, s)
                fade = power(r, (jnp.maximum(target - 1 - source, 0) * 2 * TILE).astype(f32))
                state += jnp.where(source < target, piece * fade, 0.0)
            out[i] = state.astype(bf16)


def outer_body(place, rate, inner, q, near, far, before, mixed_out, sums_out, squares):
    core, zl = place[1], place[2]
    upper = core == 1
    position = iota((TILE, D), 0).astype(f32)
    squares[...] = jnp.zeros_like(squares)
    for half, source in ((core, near), (1 - core, far)):
        for s in range(4):
            owner = jnp.bitwise_xor(zl, s)
            for i in range(2):
                h = half * (LOCAL // 2) + 2 * owner + i
                r = rate[h]
                entering = source[s, i].astype(f32)
                entering = jnp.where(upper, power(r, TILE) * entering + before[h].astype(f32), entering)
                high, low = split(entering)
                query = q[h]
                outer = (dot(query, high) + dot(query, low)) * jnp.exp(-r * position)
                mixed = inner[h] + outer
                mixed_out[h] = mixed
                squares[...] += mixed * mixed
    sums_out[...] = jnp.broadcast_to(jnp.sum(squares[...].T, axis=0, keepdims=True), (8, TILE))


def norm_body(mixed, own, s1, s2, s3, gain, out, rows):
    sums = own[...] + s1[...] + s2[...] + s3[...]
    inverse = lax.rsqrt(sums / (HEADS * D) + 1e-5)
    inverse = jnp.broadcast_to(inverse[0:1], (D, TILE)).T
    for h in range(LOCAL):
        rows[pl.ds(h, TILE, stride=LOCAL), :] = mixed[h] * inverse * gain[h : h + 1, :]
    out[...] = rows[...].reshape(TILE, LOCAL, D).astype(bf16)


def two_ways(value, steps0, steps1):
    pairs = [(2 * i + c, 2 * ((i + s) % 32) + c) for i in range(32) for c, s in ((0, steps0), (1, steps1))]
    return lax.ppermute(value, (*CHIPS, "core"), pairs)


def trade(value, axis, bits):
    return lax.ppermute(value, axis, [(i, i ^ bits) for i in range(4)])


def swap(value, axis="core"):
    return lax.ppermute(value, axis, [(0, 1), (1, 0)])


def after(value, *others):
    return lax.optimization_barrier((value, *others))[0]


def on_device(lin_q, lin_k, lin_v, decay_rate, norm_gain, soft_q, soft_k, soft_v, doc_ids, block_mask):
    x, zh, zl, core = (lax.axis_index(a) for a in ("x", "zh", "zl", "core"))
    chip = (x * 2 + zh) * 4 + zl
    place = jnp.stack([chip, core, zl, zh, x]).astype(jnp.int32)
    big = pltpu.VMEM((TILE * LOCAL, D), f32)
    heads = (LOCAL, D, D)
    pair = (2, D, D)

    block = jnp.concatenate(
        [
            jnp.transpose(soft_k, (1, 0, 2)).reshape(KV * D, D),
            jnp.transpose(soft_v, (1, 2, 0)).reshape(KV * D, D),
            jnp.broadcast_to(doc_ids.astype(bf16)[:, None], (16, D)),
        ],
        axis=0,
    )[None]
    mate = swap(block)
    both = jnp.concatenate((block, mate), axis=0)
    arrived = two_ways(both, 1, 8), two_ways(both, 9, 16)

    state_high, state = call(
        state_body, [shape(heads, bf16), shape(heads, f32)], [SMEM, VMEM, VMEM], [big, big], flops=1 << 30
    )(decay_rate, after(lin_k, both), lin_v)
    other_state = swap(state_high)
    slices = call(chip_body, [shape(pair, bf16)] * 4, [SMEM, SMEM, VMEM, VMEM])(place, decay_rate, state, other_state)
    far3, far2, far1 = (trade(slices[k], "zl", k) for k in (3, 2, 1))
    pieces = [slices[0], far1, far2, far3]

    inner, query = call(
        inner_body, [shape(heads, f32), shape(heads, bf16)], [SMEM, VMEM, VMEM, VMEM], [big] * 3, flops=1 << 30
    )(decay_rate, after(lin_q, slices[0]), lin_k, lin_v)

    row4, row4_sent = call(four_body, [shape(pair, f32), shape(pair, bf16)], [SMEM, SMEM] + [VMEM] * 4)(
        place, decay_rate, *pieces
    )
    x2, x3, x1 = (trade(row4_sent, "x", k) for k in (2, 3, 1))
    earlier = [x1, x2, x3]

    def attend(blocks, groups, **state):
        return flash(place, doc_ids, block_mask, blocks, groups, **state)

    def parts(k):
        dists = ((1 + k, 8 - k),) * 2 + ((9 + k, 16 - k),) * 2
        return [carried, swap(carried)], [(dists, False), (dists, True)]

    qt, *flow = attend([mate], [(((0, 0),), True)], first=(after(soft_q, row4_sent), block[0]))
    row4 = after(row4, flow[0])
    carried = after(jnp.concatenate(after(arrived, query, row4_sent), axis=0), flow[0], *earlier)
    chips0 = parts(0)
    carried = two_ways(carried, 1, -1)

    row_own, row_sent = call(row_body, [shape(pair, f32), shape(pair, bf16)], [SMEM, SMEM] + [VMEM] * 4)(
        place, decay_rate, row4, *earlier
    )
    row_other = swap(row_sent, "zh")
    flow = attend(*chips0, state=(qt, *after(tuple(flow), row_sent)))
    row_other = after(row_other, flow[0])
    carried = after(carried, row_other)
    chips1 = parts(1)
    carried = two_ways(carried, 1, -1)

    entering = call(entering_body, [shape(pair, bf16)] * 4, [SMEM, SMEM] + [VMEM] * 6)(
        place, decay_rate, *pieces, row_own, row_other
    )
    near = jnp.stack([entering[0]] + [trade(entering[k], "zl", k) for k in (1, 2, 3)])
    flow = attend(*chips1, state=(qt, *after(tuple(flow), entering[0])))
    near = after(near, flow[0])
    carried = after(carried, flow[0])
    chips2 = parts(2)
    carried = two_ways(carried, 1, -1)

    far = swap(near)
    mixed, sums = call(
        outer_body,
        [shape(heads, f32), shape((8, TILE), f32)],
        [SMEM, SMEM] + [VMEM] * 5,
        [pltpu.VMEM((TILE, D), f32)],
        flops=1 << 30,
    )(place, decay_rate, inner, query, near, far, other_state)
    others = [trade(sums, "head", s) for s in (1, 2, 3)]
    flow = attend(*chips2, state=(qt, *after(tuple(flow), sums)))
    carried, *flow = after((carried, *flow), *others)
    (local, swapped), (local_at, swapped_at) = parts(3)
    flow = attend([local], [local_at], state=(qt, *flow))
    soft_out = attend([swapped], [swapped_at], state=(qt, *flow), last=True)
    lin_out = call(norm_body, shape((TILE, LOCAL, D), bf16), [VMEM] * 6, [big])(
        after(mixed, soft_out), sums, *others, norm_gain
    )
    return lin_out, soft_out


def solution(mesh):
    names = ("x", "zh", "zl", "core", "head")
    fine = Mesh(mesh.devices.reshape(4, 2, 4, 2, 4), names)
    ctx = ("x", "zh", "zl", "core")
    wide = P(ctx, "head", None)
    return jax.shard_map(
        on_device,
        mesh=fine,
        in_specs=(wide, wide, wide, P("head"), P("head", None), wide, wide, wide, P(ctx), P(ctx, None)),
        out_specs=(wide, wide),
        check_vma=False,
    )
```
